32 devices in a mesh: pix: 4 (over y, core), exp: 8 (over z, x).
Axes of the slice: x: 2, y: 2, z: 4, core: 2. Of those that a mesh axis runs over, the one named last changes fastest.
Arguments:
- design: bfloat16 [200, 196608], P(None, ('pix', 'exp')), may hold values from -1 to 1
- det_weight: float32 [196608], P(('pix', 'exp')), may hold values from 0.2 to 2
- outlier_mask: int32 [2, 196608], P(None, ('pix', 'exp')), may hold values from 0 to 1
- star_owner: int32 [196608, 1], P(('pix', 'exp')), may hold values from 0 to 31; in each aligned block of 6144 rows (0 to 6143, 6144 to 12287, ...) at most 384 rows name the same one
- star_slot: int32 [196608], P(('pix', 'exp')), may hold values from 0 to 767
- coef_init: float32 [64, 2, 200], P('exp'), may hold values from -6 to 6
- star_ref: float32 [2, 24576], P(None, ('pix', 'exp')), may hold values from -24 to 24
- star_prior: float32 [24576], P(('pix', 'exp')), may hold values from 0.2 to 2
Outputs:
- coefficients: float32 [64, 2, 200], P('exp')
- star_means: float32 [2, 24576], P(None, ('pix', 'exp'))
The draws below stay inside these ranges and needn't reach their ends.
Inputs may be any that keep to these rules, and one draw needn't show every extreme that they name: `star_owner`: among the 6144 detections of one device, at most 384 name the same owner, and in every draw some device's detections name some owner exactly 384 times.
All inputs are finite; a program needn't handle non-finite values.
Results may differ from the reference program's by a relative error of at most 0.00045.
The reference program's roundings to bfloat16 on the way count: a program that leaves them out, or rounds other values in their place, can miss the bound.
Values sent between devices are 32-bit elements; how exact they have to be, the bound alone decides.
A program may use at most 64 MiB of HBM per device.

```python
import math
import jax
import jax.numpy as jnp
import numpy as np
from jax import lax

NTERM = 200
EXP_DEV = 8
ROWS_DEV = 6144
ITERS = 2
EXP_ROWS = 768
EXP_DET = 3072
DETECTIONS = 196608
EXPOSURES = 64
STAR_DEV = 768
STARS = 24576
CAP = 384
N_PIX = 4
N_EXP = 8
DEVICES = 32


def term_exponents(term_count):
    first_powers = []
    second_powers = []
    degree = 0
    while len(first_powers) < term_count:
        for exponent in range(degree, -1, -1):
            if len(first_powers) < term_count:
                first_powers.append(exponent)
                second_powers.append(degree - exponent)
        degree = degree + 1
    return (first_powers, second_powers, degree)


def power_table(position, top_degree):
    powers = [jnp.ones_like(position)]
    for exponent in range(1, top_degree):
        powers.append(powers[-1] * position)
    return powers


def draw_design(key, part):
    first_powers, second_powers, top_degree = term_exponents(NTERM)
    place_key = jax.random.fold_in(key, 11)
    across = jax.random.uniform(jax.random.fold_in(place_key, 1), (DETECTIONS,), jnp.float32, -1.0, 1.0)
    along = jax.random.uniform(jax.random.fold_in(place_key, 2), (DETECTIONS,), jnp.float32, -1.0, 1.0)
    table_across = power_table(across, top_degree)
    table_along = power_table(along, top_degree)
    rows_out = []
    for index in range(NTERM):
        first_power = first_powers[index]
        second_power = second_powers[index]
        factor = float(np.sqrt((2.0 * first_power + 1.0) * (2.0 * second_power + 1.0) / EXP_DET))
        term_row = table_across[first_power] * table_along[second_power] * factor
        rows_out.append(term_row.astype(jnp.bfloat16))
    return jnp.stack(rows_out, axis=0)


def draw_outlier_mask(key, part):
    mask_key = jax.random.fold_in(key, 23)
    classes = jax.random.randint(jax.random.fold_in(mask_key, 1), (EXPOSURES,), 0, 4)
    rounds = jnp.arange(ITERS, dtype=jnp.int32)[:, None]
    first_round = rounds == 0
    keep_counts = jnp.where(classes[None, :] == 0, jnp.where(first_round, 1, 7), jnp.where(classes[None, :] == 1, jnp.where(first_round, 7, 1), 7))
    detection = jnp.arange(DETECTIONS, dtype=jnp.int32)
    exposure = detection // ROWS_DEV % (EXPOSURES // EXP_DEV) * EXP_DEV + detection % ROWS_DEV // EXP_ROWS
    dice_rolls = jax.random.randint(jax.random.fold_in(mask_key, 2), (ITERS, DETECTIONS), 0, 8)
    return (dice_rolls < keep_counts[:, exposure]).astype(jnp.int32)


def touch_ends(array, stream_key, smallest, top_value):
    longest = array.shape.index(max(array.shape))
    spots = []
    for shift in (0, 1):
        where = [jax.random.randint(jax.random.fold_in(stream_key, axis), (), 0, length) for axis, length in enumerate(array.shape)]
        where[longest] = (where[longest] + shift) % array.shape[longest]
        spots.append(tuple(where))
    return array.at[spots[0]].set(smallest).at[spots[1]].set(top_value)


def steps_of(stream_key, dims, pieces, low, top_value):
    level, own = 1.0, jax.random.fold_in(stream_key, 6)
    for dim, parts in pieces:
        draws = jnp.exp(jax.random.uniform(jax.random.fold_in(own, dim), (parts,), jnp.float32, low / len(pieces), top_value / len(pieces)))
        level = level * jnp.repeat(draws, dims[dim] // parts).reshape([-1 if axis == dim else 1 for axis in range(len(dims))])
    return level


def assign_block(stream_key, own, number, rows, amount, top, reach, slope):
    order = jax.random.permutation(stream_key, amount)
    crowded, common = load_shares(amount, rows * top, reach, slope, True), load_shares(amount, rows * top, reach, slope, False)
    places = jnp.arange(amount)

    def named(sizes, rotation):
        used = int((sizes > 0).sum())
        fixed = max(1, used // 4)
        passed = fixed + (places - fixed + rotation * (used - fixed)) % max(1, amount - fixed)
        return jnp.zeros((amount,), jnp.int32).at[order[jnp.where(places < fixed, places, passed)]].set(jnp.asarray(sizes, jnp.int32))

    sizes = jnp.where(number % 4 == 0, named(crowded, number // 4), named(common, number - number // 4 - 1))
    mixed = jax.random.permutation(jax.random.fold_in(own, 3), amount)
    source_of, taker = mixed[0:amount // 2 * 2:2], mixed[1:amount // 2 * 2:2]
    slack = jnp.minimum(sizes[source_of] - 1, reach - sizes[taker]) // 2
    slack = jnp.where((source_of == order[0]) | (taker == order[0]) | (sizes[taker] == 0), 0, jnp.maximum(slack, 0))
    passed = jax.random.randint(jax.random.fold_in(own, 4), (amount // 2,), 0, 1 << 20) % (slack + 1)
    sizes = sizes.at[source_of].add(-passed).at[taker].add(passed)
    labels = jnp.searchsorted(jnp.cumsum(sizes), jnp.arange(rows * top), side="right").astype(jnp.int32)
    grid = labels.reshape(top, rows).T
    grid = grid[jax.random.permutation(jax.random.fold_in(own, 1), rows)]
    rotation = jax.random.randint(jax.random.fold_in(own, 2), (rows, 1), 0, top)
    return jnp.take_along_axis(grid, (jnp.arange(top)[None, :] + rotation) % top, axis=1)


def load_shares(number_of, total, reach, lean, full):
    weights = [(1 << 20) // math.isqrt(grade ** lean) + 1 for grade in range(1, number_of + 1)]
    largest = reach if full else min(reach, max(-(-total // number_of), total * weights[0] // sum(weights)))
    least = 1 if total - largest >= number_of - 1 else 0
    counts, surplus = [largest] + [least] * (number_of - 1), total - largest - least * (number_of - 1)
    while surplus > 0:
        movable = [i for i in range(1, number_of) if counts[i] < largest] or [i for i in range(1, number_of) if counts[i] < reach]
        mass, left = sum([weights[i] for i in movable]), surplus
        for i in movable:
            extra = min(reach - counts[i], max(1, left * weights[i] // mass), surplus)
            counts[i] = counts[i] + extra
            surplus = surplus - extra
    return np.array(counts)


def gaussian(rng, dims, spread, reach, split=(), held_as=jnp.bfloat16):
    entries = jax.random.normal(rng, dims, jnp.float32) * spread
    if len(split) > 0:
        entries = steps_of(rng, dims, split, -0.22, 0.18) * entries
    return jnp.clip(entries, min=-reach, max=reach).astype(held_as)


def setup_inputs(seed: int = 0) -> dict:
    key_list = jax.random.split(jax.random.key(seed), 9)
    design = draw_design(jax.random.fold_in(key_list[8], 71), 0)
    det_weight = jnp.clip(jnp.exp(math.log(2.0) - 2.3025851 * jax.random.uniform(key_list[1], (DETECTIONS,), jnp.float32) ** steps_of(key_list[1], (DETECTIONS,), ((0, 32),), -0.2, 0.2)), 0.2, 2.0)
    outlier_mask = draw_outlier_mask(jax.random.fold_in(key_list[8], 71), 0)
    star_owner_keys = jax.random.split(jax.random.fold_in(key_list[3], 1), DETECTIONS // ROWS_DEV)
    star_owner_turns = jax.random.permutation(jax.random.fold_in(key_list[3], 3), DETECTIONS // ROWS_DEV)
    star_owner = jax.vmap(lambda own, number: assign_block(jax.random.fold_in(key_list[3], 2), own, number, ROWS_DEV, DEVICES, 1, CAP, 2))(star_owner_keys, star_owner_turns).reshape((DETECTIONS, 1))
    star_slot = touch_ends(jax.random.randint(key_list[4], (DETECTIONS,), 0, STAR_DEV), jax.random.fold_in(key_list[4], 1), 0, STAR_DEV - 1).astype(jnp.int32)
    coef_init = gaussian(key_list[5], (EXPOSURES, 2, NTERM), 1.0, 6.0, ((0, 8),), jnp.float32)
    star_ref = gaussian(key_list[6], (2, STARS), 4.0, 24.0, ((1, 32),), jnp.float32)
    star_prior = jnp.clip(jnp.exp(math.log(2.0) - 2.3025851 * jax.random.uniform(key_list[7], (STARS,), jnp.float32) ** steps_of(key_list[7], (STARS,), ((0, 32),), -0.2, 0.2)), 0.2, 2.0)
    return {"design": design, "det_weight": det_weight, "outlier_mask": outlier_mask, "star_owner": star_owner, "star_slot": star_slot, "coef_init": coef_init, "star_ref": star_ref, "star_prior": star_prior}


RIDGE = 0.5

def solve_blocks(gram_block, right_side):
    identity = jnp.eye(gram_block.shape[-1], dtype=jnp.float32)
    factor = jnp.linalg.cholesky(gram_block + RIDGE * identity)
    columns = jnp.swapaxes(right_side, 1, 2)
    middle = jax.scipy.linalg.solve_triangular(factor, columns, lower=True)
    update = jax.scipy.linalg.solve_triangular(factor, middle, lower=True, trans=1)
    return jnp.swapaxes(update, 1, 2)

def reference(design, det_weight, outlier_mask, star_owner, star_slot, coef_init, star_ref, star_prior):
    blocks = N_PIX * N_EXP
    star_index = star_owner[:, 0] * STAR_DEV + star_slot
    block_ids = jnp.arange(blocks, dtype=jnp.int32)
    coefficients = coef_init
    star_means = jnp.zeros((2, STARS), jnp.float32)
    for step_index in range(ITERS):
        maps_lo = coefficients.astype(jnp.bfloat16)
        masked_weight = det_weight * outlier_mask[step_index].astype(jnp.float32)

        def predict(block_index):
            columns = lax.dynamic_slice_in_dim(design, block_index * ROWS_DEV, ROWS_DEV, 1)
            exp_group = block_index % N_EXP
            local_maps = lax.dynamic_slice_in_dim(maps_lo, exp_group * EXP_DEV, EXP_DEV, 0)
            shaped = columns.astype(jnp.float32).reshape(NTERM, EXP_DEV, EXP_ROWS)
            result = jnp.einsum('jct,tjr->cjr', local_maps.astype(jnp.float32), shaped)
            return result.reshape(2, ROWS_DEV)
        predicted = lax.map(predict, block_ids)
        predicted = jnp.swapaxes(predicted, 0, 1).reshape(2, blocks * ROWS_DEV)
        numerator = jnp.zeros((2, STARS), jnp.float32).at[:, star_index].add(masked_weight[None, :] * predicted)
        denominator = jnp.zeros((STARS,), jnp.float32).at[star_index].add(masked_weight)
        star_means = (star_prior * star_ref + numerator) / (star_prior + denominator)
        residual_lo = (star_means[:, star_index] - predicted).astype(jnp.bfloat16)

        def normal(block_index):
            columns = lax.dynamic_slice_in_dim(design, block_index * ROWS_DEV, ROWS_DEV, 1)
            weight_block = lax.dynamic_slice_in_dim(masked_weight, block_index * ROWS_DEV, ROWS_DEV, 0)
            residual_block = lax.dynamic_slice_in_dim(residual_lo, block_index * ROWS_DEV, ROWS_DEV, 1)
            design_wide = columns.astype(jnp.float32)
            weighted = (design_wide * weight_block[None, :]).astype(jnp.bfloat16)
            weighted_wide = weighted.astype(jnp.float32).reshape(NTERM, EXP_DEV, EXP_ROWS)
            design_wide = design_wide.reshape(NTERM, EXP_DEV, EXP_ROWS)
            gram_block = jnp.einsum('tjr,ujr->jtu', weighted_wide, design_wide)
            residual_wide = residual_block.astype(jnp.float32).reshape(2, EXP_DEV, EXP_ROWS)
            right_side = jnp.einsum('tjr,cjr->jct', weighted_wide, residual_wide)
            return (gram_block, right_side)
        gram_blocks, right_sides = lax.map(normal, block_ids)
        gram_blocks = gram_blocks.reshape(N_PIX, EXPOSURES, NTERM, NTERM).sum(axis=0)
        right_sides = right_sides.reshape(N_PIX, EXPOSURES, 2, NTERM).sum(axis=0)
        coefficients = coefficients + solve_blocks(gram_blocks, right_sides)
    return (coefficients, star_means)
```

```python
import functools

import jax
import jax.numpy as jnp
from jax import lax
from jax.experimental import pallas as pl
from jax.experimental.pallas import tpu as pltpu
from jax.sharding import PartitionSpec as P

ITERS = 2
RIDGE = 0.5
LANES = 128
PIVOTS = 40
VMEM_BYTES = 50 * 1024 * 1024


def split_two(x):
    high = x.astype(jnp.bfloat16)
    low = (x - high.astype(jnp.float32)).astype(jnp.bfloat16)
    return high, low


def slot_table(slot_row, star_count):
    ids = lax.broadcasted_iota(jnp.int32, (star_count, slot_row.shape[1]), 0)
    return jnp.where(ids == slot_row, 1.0, 0.0).astype(jnp.bfloat16)


def dot_last(a, b):
    return lax.dot_general(a, b, (((1,), (1,)), ((), ())), preferred_element_type=jnp.float32)


def scatter_block(values, owner_row, slot_row, peers, star_count):
    hot = lax.broadcasted_iota(jnp.int32, (peers, owner_row.shape[1]), 0) == owner_row
    parts = []
    for value in values:
        high = value.astype(jnp.bfloat16).astype(jnp.float32)
        for part in (high, value - high):
            parts.append(jnp.where(hot, part, 0.0).astype(jnp.bfloat16))
    table = slot_table(slot_row, star_count)
    return dot_last(jnp.concatenate(parts, axis=0), table)


def sums_kernel(
    peers, chosen, design_ref, weight_ref, mask_ref, owner_ref, slot_ref, coef_ref, *out_refs
):
    predicted_ref, sums_ref = out_refs[-2:]
    maps_device = coef_ref.shape[0]
    width = design_ref.shape[1] // maps_device
    count, _, star_count = sums_ref.shape

    def block(j, total):
        at = pl.ds(pl.multiple_of(j * width, width), width)
        design = design_ref[:, at]
        weights = [weight_ref[:, at] * mask_ref[k : k + 1, at].astype(jnp.float32) for k in chosen]
        if len(chosen) > 1:
            wide = design.astype(jnp.float32)
            for k in range(len(chosen)):
                weighted = (wide * weights[k]).astype(jnp.bfloat16)
                out_refs[0][k, j] = dot_last(weighted, design)
        maps = coef_ref[j].astype(jnp.bfloat16)
        predicted = jnp.dot(maps, design, preferred_element_type=jnp.float32)
        predicted_ref[:, at] = predicted
        values = [predicted[c : c + 1] * weights[0] for c in range(2)]
        if len(chosen) > 1:
            values = values + weights
        return total + scatter_block(
            values, owner_ref[:, at], slot_ref[:, at], peers, star_count
        )

    total = lax.fori_loop(
        0, maps_device, block, jnp.zeros((2 * count * peers, star_count), jnp.float32)
    )
    for v in range(count):
        at = 2 * v * peers
        sums_ref[v] = total[at : at + peers] + total[at + peers : at + 2 * peers]


def right_kernel(
    peers, design_ref, weight_ref, mask_ref, owner_ref, slot_ref, predicted_ref, means_ref,
    right_ref, split_ref,
):
    @pl.when(pl.program_id(0) == 0)
    def _():
        for c in range(2):
            high, low = split_two(means_ref[c])
            split_ref[2 * c * peers : (2 * c + 1) * peers] = high
            split_ref[(2 * c + 1) * peers : (2 * c + 2) * peers] = low

    owner_row = owner_ref[...]
    table = slot_table(slot_ref[...], split_ref.shape[1])
    found = jnp.dot(split_ref[...], table, preferred_element_type=jnp.float32)
    hot = lax.broadcasted_iota(jnp.int32, (peers, owner_row.shape[1]), 0) == owner_row
    rows = []
    for c in range(2):
        at = 2 * c * peers
        both = found[at : at + peers] + found[at + peers : at + 2 * peers]
        mean = jnp.sum(jnp.where(hot, both, 0.0), axis=0, keepdims=True)
        rows.append(mean - predicted_ref[c : c + 1, :])
    residual = jnp.concatenate(rows, axis=0).astype(jnp.bfloat16)
    weight = weight_ref[...] * mask_ref[...].astype(jnp.float32)
    weighted = (design_ref[...].astype(jnp.float32) * weight).astype(jnp.bfloat16)
    right_ref[0] = dot_last(residual, weighted)


def sweep_panel(panels):
    lane = lax.broadcasted_iota(jnp.int32, (8, LANES), 1)
    row = lax.broadcasted_iota(jnp.int32, (8, LANES), 0)
    for s in range(PIVOTS):
        tile, sub = s // 8, s % 8
        swept = []
        for panel in panels:
            columns = [jnp.broadcast_to(t[0][:, s : s + 1], (8, LANES)) for t in panel]
            pivot = jnp.broadcast_to(columns[tile][sub : sub + 1, :], (8, LANES))
            inverse = 1.0 / pivot
            fresh = [
                jnp.broadcast_to(half[sub : sub + 1, :], (8, LANES)) * inverse
                for half in panel[tile]
            ]
            fresh[0] = jnp.where(lane == s, -inverse, fresh[0])
            done = []
            for t in range(len(panel)):
                halves = []
                for h in range(len(panel[t])):
                    old = jnp.where(lane == s, 0.0, panel[t][h]) if h == 0 else panel[t][h]
                    new = old - columns[t] * fresh[h]
                    if t == tile:
                        new = jnp.where(row == sub, fresh[h], new)
                    halves.append(new)
                done.append(halves)
            swept.append(done)
        panels = swept
    return panels


def inverse_kernel(gram_ref, out_ref, work_ref):
    count, size = gram_ref.shape[0], gram_ref.shape[1]
    span = work_ref.shape[2]
    tiles = PIVOTS // 8
    halves = span // LANES
    diagonal = lax.broadcasted_iota(jnp.int32, (size, size), 0) == lax.broadcasted_iota(
        jnp.int32, (size, size), 1
    )
    work_ref[...] = jnp.zeros_like(work_ref)
    for m in range(count):
        gram = gram_ref[m]
        work_ref[m, :size, :size] = 0.5 * (gram + gram.T) + jnp.where(diagonal, RIDGE, 0.0)

    def block(_, carry):
        panels = [
            [
                [work_ref[m, 8 * t : 8 * t + 8, LANES * h : LANES * (h + 1)] for h in range(halves)]
                for t in range(tiles)
            ]
            for m in range(count)
        ]
        swept = sweep_panel(panels)
        for m in range(count):
            before = work_ref[m, :PIVOTS, :]
            after = jnp.concatenate(
                [jnp.concatenate(tile, axis=1) for tile in swept[m]], axis=0
            )
            change = lax.dot_general(
                before, after, (((0,), (0,)), ((), ())),
                precision=lax.Precision.HIGHEST, preferred_element_type=jnp.float32,
            )
            lanes = lax.broadcasted_iota(jnp.int32, (span - PIVOTS, span), 1)
            rest = jnp.where(lanes < PIVOTS, 0.0, work_ref[m, PIVOTS:, :]) - change[PIVOTS:, :]
            work_ref[m, : span - PIVOTS, :] = pltpu.roll(rest, span - PIVOTS, 1)
            work_ref[m, span - PIVOTS :, :] = pltpu.roll(after, span - PIVOTS, 1)
        return carry

    lax.fori_loop(0, size // PIVOTS, block, 0)
    start = span - size
    for m in range(count):
        turned = pltpu.roll(work_ref[m, start:, :], size, 1)
        out_ref[m] = -turned[:, :size]


def invert(grams):
    count, size = grams.shape[0], grams.shape[1]
    span = -(-size // LANES) * LANES
    return pl.pallas_call(
        inverse_kernel,
        out_shape=jax.ShapeDtypeStruct((count, size, size), jnp.float32),
        in_specs=[pl.BlockSpec(memory_space=pltpu.VMEM)],
        out_specs=pl.BlockSpec(memory_space=pltpu.VMEM),
        scratch_shapes=[pltpu.VMEM((count, span, span), jnp.float32)],
        compiler_params=pltpu.CompilerParams(vmem_limit_bytes=VMEM_BYTES),
    )(grams)


def on_device(
    design, det_weight, outlier_mask, star_owner, star_slot, coef_init, star_ref, star_prior
):
    highest = lax.Precision.HIGHEST
    peers = lax.axis_size(("pix", "exp"))
    pix_count = lax.axis_size("pix")
    terms, rows = design.shape
    maps_device = coef_init.shape[0]
    width = rows // maps_device
    star_count = star_prior.shape[0]
    share = maps_device // pix_count
    weight_row = det_weight.reshape(1, rows)
    owner_row = star_owner.reshape(1, rows)
    slot_row = star_slot.reshape(1, rows)
    params = pltpu.CompilerParams(vmem_limit_bytes=VMEM_BYTES)

    def line(count):
        return pl.BlockSpec((count, width), lambda j: (0, j))

    maps_spec = pl.BlockSpec((1, 2, terms), lambda j: (j, 0, 0))

    def whole(shape):
        return pl.BlockSpec(shape, lambda j: (0,) * len(shape))

    f32 = jnp.float32
    def sums_call(chosen, coefficients):
        count = 2 + (len(chosen) if len(chosen) > 1 else 0)
        shapes = [
            jax.ShapeDtypeStruct((2, rows), f32),
            jax.ShapeDtypeStruct((count, peers, star_count), f32),
        ]
        if len(chosen) > 1:
            shapes.insert(0, jax.ShapeDtypeStruct((ITERS, maps_device, terms, terms), f32))
        vmem = pl.BlockSpec(memory_space=pltpu.VMEM)
        return pl.pallas_call(
            functools.partial(sums_kernel, peers, chosen),
            out_shape=tuple(shapes),
            in_specs=[vmem] * 6,
            out_specs=(vmem,) * len(shapes),
            compiler_params=params,
        )(design, weight_row, outlier_mask, owner_row, slot_row, coefficients)

    grams, predicted, sums = sums_call(tuple(range(ITERS)), coef_init)
    own_grams = lax.psum_scatter(grams, "pix", scatter_dimension=1, tiled=True)
    inverses = invert(own_grams.reshape(ITERS * share, terms, terms)).reshape(own_grams.shape)
    coefficients = coef_init
    bottoms = None
    for k in range(ITERS):
        mask_row = outlier_mask[k : k + 1]
        if k > 0:
            predicted, sums = sums_call((k,), coefficients)
        arrived = lax.all_to_all(
            sums, ("pix", "exp"), split_axis=1, concat_axis=1, tiled=True
        )
        totals = jnp.sum(arrived, axis=1)
        if k == 0:
            bottoms = totals[2:]
        star_means = (star_prior * star_ref + totals[:2]) / (star_prior + bottoms[k])
        all_means = lax.all_gather(star_means, ("pix", "exp"), axis=1, tiled=False)
        right = pl.pallas_call(
            functools.partial(right_kernel, peers),
            grid=(maps_device,),
            out_shape=jax.ShapeDtypeStruct((maps_device, 2, terms), f32),
            in_specs=[
                line(terms), line(1), line(1), line(1), line(1), line(2),
                whole((2, peers, star_count)),
            ],
            out_specs=maps_spec,
            scratch_shapes=[pltpu.VMEM((4 * peers, star_count), jnp.bfloat16)],
            compiler_params=params,
        )(design, weight_row, mask_row, owner_row, slot_row, predicted, all_means)
        own_right = lax.psum_scatter(right, "pix", scatter_dimension=0, tiled=True)
        own_maps = lax.dynamic_slice_in_dim(
            coefficients, lax.axis_index("pix") * share, share, 0
        )
        update = jnp.einsum("ect,etu->ecu", own_right, inverses[k], precision=highest)
        coefficients = lax.all_gather(own_maps + update, "pix", axis=0, tiled=True)
    return (coefficients, star_means)


def solution(mesh):
    placed = (
        P(None, ("pix", "exp")),
        P(("pix", "exp")),
        P(None, ("pix", "exp")),
        P(("pix", "exp"), None),
        P(("pix", "exp")),
        P("exp", None, None),
        P(None, ("pix", "exp")),
        P(("pix", "exp")),
    )
    return jax.shard_map(
        on_device,
        mesh=mesh,
        in_specs=placed,
        out_specs=(P("exp", None, None), P(None, ("pix", "exp"))),
        check_vma=False,
    )
```

```python
import functools

import jax
import jax.numpy as jnp
from jax import lax
from jax.experimental import pallas as pl
from jax.experimental.pallas import tpu as pltpu
from jax.sharding import PartitionSpec as P

ITERS = 2
RIDGE = 0.5
LANES = 128
PIVOTS = 40
VMEM_BYTES = 50 * 1024 * 1024


def split_two(x):
    high = x.astype(jnp.bfloat16)
    low = (x - high.astype(jnp.float32)).astype(jnp.bfloat16)
    return high, low


def slot_table(slot_row, star_count):
    ids = lax.broadcasted_iota(jnp.int32, (star_count, slot_row.shape[1]), 0)
    return jnp.where(ids == slot_row, 1.0, 0.0).astype(jnp.bfloat16)


def dot_last(a, b):
    return lax.dot_general(a, b, (((1,), (1,)), ((), ())), preferred_element_type=jnp.float32)


def scatter_block(values, owner_row, slot_row, peers, star_count):
    hot = lax.broadcasted_iota(jnp.int32, (peers, owner_row.shape[1]), 0) == owner_row
    parts = []
    for value in values:
        high = value.astype(jnp.bfloat16).astype(jnp.float32)
        for part in (high, value - high):
            parts.append(jnp.where(hot, part, 0.0).astype(jnp.bfloat16))
    table = slot_table(slot_row, star_count)
    return dot_last(jnp.concatenate(parts, axis=0), table)


def sums_kernel(
    peers, chosen, design_ref, weight_ref, mask_ref, owner_ref, slot_ref, coef_ref, *out_refs
):
    predicted_ref, sums_ref = out_refs[-2:]
    maps_device = coef_ref.shape[0]
    width = design_ref.shape[1] // maps_device
    count, _, star_count = sums_ref.shape

    def block(j, total):
        at = pl.ds(pl.multiple_of(j * width, width), width)
        design = design_ref[:, at]
        weights = [weight_ref[:, at] * mask_ref[k : k + 1, at].astype(jnp.float32) for k in chosen]
        if len(chosen) > 1:
            wide = design.astype(jnp.float32)
            for k in range(len(chosen)):
                weighted = (wide * weights[k]).astype(jnp.bfloat16)
                out_refs[0][k, j] = dot_last(weighted, design)
        maps = coef_ref[j].astype(jnp.bfloat16)
        predicted = jnp.dot(maps, design, preferred_element_type=jnp.float32)
        predicted_ref[:, at] = predicted
        values = [predicted[c : c + 1] * weights[0] for c in range(2)]
        if len(chosen) > 1:
            values = values + weights
        return total + scatter_block(
            values, owner_ref[:, at], slot_ref[:, at], peers, star_count
        )

    total = lax.fori_loop(
        0, maps_device, block, jnp.zeros((2 * count * peers, star_count), jnp.float32)
    )
    for v in range(count):
        at = 2 * v * peers
        sums_ref[v] = total[at : at + peers] + total[at + peers : at + 2 * peers]


def right_kernel(
    peers, design_ref, weight_ref, mask_ref, owner_ref, slot_ref, predicted_ref, means_ref,
    right_ref, split_ref,
):
    @pl.when(pl.program_id(0) == 0)
    def _():
        for c in range(2):
            high, low = split_two(means_ref[c])
            split_ref[2 * c * peers : (2 * c + 1) * peers] = high
            split_ref[(2 * c + 1) * peers : (2 * c + 2) * peers] = low

    owner_row = owner_ref[...]
    table = slot_table(slot_ref[...], split_ref.shape[1])
    found = jnp.dot(split_ref[...], table, preferred_element_type=jnp.float32)
    hot = lax.broadcasted_iota(jnp.int32, (peers, owner_row.shape[1]), 0) == owner_row
    rows = []
    for c in range(2):
        at = 2 * c * peers
        both = found[at : at + peers] + found[at + peers : at + 2 * peers]
        mean = jnp.sum(jnp.where(hot, both, 0.0), axis=0, keepdims=True)
        rows.append(mean - predicted_ref[c : c + 1, :])
    residual = jnp.concatenate(rows, axis=0).astype(jnp.bfloat16)
    weight = weight_ref[...] * mask_ref[...].astype(jnp.float32)
    weighted = (design_ref[...].astype(jnp.float32) * weight).astype(jnp.bfloat16)
    right_ref[0] = dot_last(residual, weighted)


def sweep_panel(panels):
    lane = lax.broadcasted_iota(jnp.int32, (8, LANES), 1)
    row = lax.broadcasted_iota(jnp.int32, (8, LANES), 0)
    for s in range(PIVOTS):
        tile, sub = s // 8, s % 8
        swept = []
        for panel in panels:
            columns = [jnp.broadcast_to(t[0][:, s : s + 1], (8, LANES)) for t in panel]
            pivot = jnp.broadcast_to(columns[tile][sub : sub + 1, :], (8, LANES))
            inverse = 1.0 / pivot
            fresh = [
                jnp.broadcast_to(half[sub : sub + 1, :], (8, LANES)) * inverse
                for half in panel[tile]
            ]
            fresh[0] = jnp.where(lane == s, -inverse, fresh[0])
            done = []
            for t in range(len(panel)):
                halves = []
                for h in range(len(panel[t])):
                    old = jnp.where(lane == s, 0.0, panel[t][h]) if h == 0 else panel[t][h]
                    new = old - columns[t] * fresh[h]
                    if t == tile:
                        new = jnp.where(row == sub, fresh[h], new)
                    halves.append(new)
                done.append(halves)
            swept.append(done)
        panels = swept
    return panels


def inverse_kernel(gram_ref, out_ref, work_ref):
    count, size = gram_ref.shape[0], gram_ref.shape[1]
    span = work_ref.shape[2]
    tiles = PIVOTS // 8
    halves = span // LANES
    diagonal = lax.broadcasted_iota(jnp.int32, (size, size), 0) == lax.broadcasted_iota(
        jnp.int32, (size, size), 1
    )
    work_ref[...] = jnp.zeros_like(work_ref)
    for m in range(count):
        gram = gram_ref[m]
        work_ref[m, :size, :size] = 0.5 * (gram + gram.T) + jnp.where(diagonal, RIDGE, 0.0)

    def block(_, carry):
        panels = [
            [
                [work_ref[m, 8 * t : 8 * t + 8, LANES * h : LANES * (h + 1)] for h in range(halves)]
                for t in range(tiles)
            ]
            for m in range(count)
        ]
        swept = sweep_panel(panels)
        for m in range(count):
            before = work_ref[m, :PIVOTS, :]
            after = jnp.concatenate(
                [jnp.concatenate(tile, axis=1) for tile in swept[m]], axis=0
            )
            change = lax.dot_general(
                before, after, (((0,), (0,)), ((), ())),
                precision=lax.Precision.HIGHEST, preferred_element_type=jnp.float32,
            )
            lanes = lax.broadcasted_iota(jnp.int32, (span - PIVOTS, span), 1)
            rest = jnp.where(lanes < PIVOTS, 0.0, work_ref[m, PIVOTS:, :]) - change[PIVOTS:, :]
            work_ref[m, : span - PIVOTS, :] = pltpu.roll(rest, span - PIVOTS, 1)
            work_ref[m, span - PIVOTS :, :] = pltpu.roll(after, span - PIVOTS, 1)
        return carry

    lax.fori_loop(0, size // PIVOTS, block, 0)
    start = span - size
    for m in range(count):
        turned = pltpu.roll(work_ref[m, start:, :], size, 1)
        out_ref[m] = -turned[:, :size]


def invert(grams):
    count, size = grams.shape[0], grams.shape[1]
    span = -(-size // LANES) * LANES
    return pl.pallas_call(
        inverse_kernel,
        out_shape=jax.ShapeDtypeStruct((count, size, size), jnp.float32),
        in_specs=[pl.BlockSpec(memory_space=pltpu.VMEM)],
        out_specs=pl.BlockSpec(memory_space=pltpu.VMEM),
        scratch_shapes=[pltpu.VMEM((count, span, span), jnp.float32)],
        compiler_params=pltpu.CompilerParams(vmem_limit_bytes=VMEM_BYTES),
    )(grams)


def on_device(
    design, det_weight, outlier_mask, star_owner, star_slot, coef_init, star_ref, star_prior
):
    highest = lax.Precision.HIGHEST
    peers = lax.axis_size(("pix", "exp"))
    pix_count = lax.axis_size("pix")
    terms, rows = design.shape
    maps_device = coef_init.shape[0]
    width = rows // maps_device
    star_count = star_prior.shape[0]
    share = maps_device // pix_count
    weight_row = det_weight.reshape(1, rows)
    owner_row = star_owner.reshape(1, rows)
    slot_row = star_slot.reshape(1, rows)
    params = pltpu.CompilerParams(vmem_limit_bytes=VMEM_BYTES)

    def line(count):
        return pl.BlockSpec((count, width), lambda j: (0, j))

    maps_spec = pl.BlockSpec((1, 2, terms), lambda j: (j, 0, 0))

    def whole(shape):
        return pl.BlockSpec(shape, lambda j: (0,) * len(shape))

    f32 = jnp.float32
    def sums_call(chosen, coefficients):
        count = 2 + (len(chosen) if len(chosen) > 1 else 0)
        shapes = [
            jax.ShapeDtypeStruct((2, rows), f32),
            jax.ShapeDtypeStruct((count, peers, star_count), f32),
        ]
        if len(chosen) > 1:
            shapes.insert(0, jax.ShapeDtypeStruct((ITERS, maps_device, terms, terms), f32))
        vmem = pl.BlockSpec(memory_space=pltpu.VMEM)
        return pl.pallas_call(
            functools.partial(sums_kernel, peers, chosen),
            out_shape=tuple(shapes),
            in_specs=[vmem] * 6,
            out_specs=(vmem,) * len(shapes),
            compiler_params=params,
        )(design, weight_row, outlier_mask, owner_row, slot_row, coefficients)

    grams, predicted, sums = sums_call(tuple(range(ITERS)), coef_init)
    own_grams = lax.psum_scatter(grams, "pix", scatter_dimension=1, tiled=True)
    inverses = invert(own_grams.reshape(ITERS * share, terms, terms)).reshape(own_grams.shape)
    coefficients = coef_init
    bottoms = None
    for k in range(ITERS):
        mask_row = outlier_mask[k : k + 1]
        if k > 0:
            predicted, sums = sums_call((k,), coefficients)
        arrived = lax.all_to_all(
            sums, ("pix", "exp"), split_axis=1, concat_axis=1, tiled=True
        )
        totals = jnp.sum(arrived, axis=1)
        if k == 0:
            bottoms = totals[2:]
        star_means = (star_prior * star_ref + totals[:2]) / (star_prior + bottoms[k])
        copies = jnp.broadcast_to(star_means[:, None, :], (2, peers, star_count))
        all_means = lax.all_to_all(
            copies, ("pix", "exp"), split_axis=1, concat_axis=1, tiled=True
        )
        right = pl.pallas_call(
            functools.partial(right_kernel, peers),
            grid=(maps_device,),
            out_shape=jax.ShapeDtypeStruct((maps_device, 2, terms), f32),
            in_specs=[
                line(terms), line(1), line(1), line(1), line(1), line(2),
                whole((2, peers, star_count)),
            ],
            out_specs=maps_spec,
            scratch_shapes=[pltpu.VMEM((4 * peers, star_count), jnp.bfloat16)],
            compiler_params=params,
        )(design, weight_row, mask_row, owner_row, slot_row, predicted, all_means)
        own_right = lax.psum_scatter(right, "pix", scatter_dimension=0, tiled=True)
        own_maps = lax.dynamic_slice_in_dim(
            coefficients, lax.axis_index("pix") * share, share, 0
        )
        update = jnp.einsum("ect,etu->ecu", own_right, inverses[k], precision=highest)
        coefficients = lax.all_gather(own_maps + update, "pix", axis=0, tiled=True)
    return (coefficients, star_means)


def solution(mesh):
    placed = (
        P(None, ("pix", "exp")),
        P(("pix", "exp")),
        P(None, ("pix", "exp")),
        P(("pix", "exp"), None),
        P(("pix", "exp")),
        P("exp", None, None),
        P(None, ("pix", "exp")),
        P(("pix", "exp")),
    )
    return jax.shard_map(
        on_device,
        mesh=mesh,
        in_specs=placed,
        out_specs=(P("exp", None, None), P(None, ("pix", "exp"))),
        check_vma=False,
    )
```
